32 devices in a mesh: layer: 4 (over y, x), head: 8 (over z, core).
Axes of the slice: x: 2, y: 2, z: 4, core: 2. Of those that a mesh axis runs over, the one named last changes fastest.
Arguments:
- momentum: bfloat16 [4, 32768, 512], P(None, ('layer', 'head')), may hold values from -6 to 6
- grad_one: bfloat16 [4, 32768, 512], P(None, ('layer', 'head')), may hold values from -6 to 6
- grad_two: bfloat16 [4, 32768, 512], P(None, ('layer', 'head')), may hold values from -60 to 60
Outputs:
- update_one: float32 [4, 32768, 512], P(None, ('layer', 'head'))
- update_two: float32 [4, 32768, 512], P(None, ('layer', 'head'))
The draws below stay inside these ranges and needn't reach their ends.
All inputs are finite; a program needn't handle non-finite values.
Results may differ from the reference program's by a relative error of at most 0.0065.
Values may be sent and summed in bfloat16 or wider, within the bound.
No kernel may reach another device: no remote copies, remote signals or barrier semaphores. Data moves between devices by JAX's collectives and lax.ppermute only.
A program may use at most 128 MiB of HBM per device.

```python
import jax
import jax.numpy as jnp
from jax import lax

LATENT = 512
HEADS = 128
HEAD_ROWS = 256
NS_ITERS = 5
ROWS = 32768
LAYERS = 4
N_HEAD = 8
DEVICES = 32


def draw_grad_two(key, part):
    row_index = jnp.arange(ROWS, dtype=jnp.int32)
    block_index = row_index // (ROWS // DEVICES) % N_HEAD
    position = block_index.astype(jnp.float32) / jnp.float32(max(N_HEAD - 1, 1))
    scales = jnp.exp(jnp.log(jnp.float32(8.0)) * position)
    values = jnp.clip(jax.random.normal(key, (LAYERS, ROWS, LATENT), jnp.float32), -6.0, 6.0)
    return (values * scales[None, :, None]).astype(jnp.bfloat16)


def steps_of(rng, extent, pieces, least, largest):
    factor_of = 1.0
    for dim, blocks in pieces:
        heights = jax.random.uniform(jax.random.fold_in(jax.random.fold_in(rng, 6), dim), (blocks,), jnp.float32, least / len(pieces), largest / len(pieces))
        factor_of = factor_of * jnp.repeat(jnp.exp(heights), extent[dim] // blocks).reshape((-1,) + (1,) * (len(extent) - 1 - dim))
    return factor_of


def scatter_about(rng, extent, width, limit, shards=(), kind=jnp.bfloat16):
    array = width * jax.random.normal(rng, extent, jnp.float32)
    if shards:
        array = array * steps_of(rng, extent, shards, -0.22, 0.18)
    return jnp.clip(array, -limit, limit).astype(kind)


def setup_inputs(seed: int = 0) -> dict:
    key_of = jax.random.split(jax.random.key(seed), 4)
    momentum = scatter_about(key_of[0], (LAYERS, ROWS, LATENT), 1.0, 6.0, ((1, 32),))
    grad_one = scatter_about(key_of[1], (LAYERS, ROWS, LATENT), 1.0, 6.0, ((1, 32),))
    grad_two = draw_grad_two(jax.random.fold_in(key_of[3], 71), 0)
    return dict(momentum=momentum, grad_one=grad_one, grad_two=grad_two)


quintic_a = 3.4445
quintic_b = -4.775
quintic_c = 2.0315
norm_epsilon = 1e-07
momentum_decay = 0.95

def block_newton(blocks):
    wide = blocks.astype(jnp.float32)
    squares = lax.optimization_barrier(jnp.sum(jnp.square(wide), axis=(1, 2), keepdims=True))
    current = wide / (jnp.sqrt(squares) + norm_epsilon)
    for iteration in range(NS_ITERS):
        gram_part = jnp.einsum('nrl,nsl->nrs', current, current, precision=lax.Precision.HIGHEST)
        polynomial = quintic_b * gram_part + quintic_c * jnp.einsum('nrs,nst->nrt', gram_part, gram_part, precision=lax.Precision.HIGHEST)
        current = quintic_a * current + jnp.einsum('nrs,nsl->nrl', polynomial, current, precision=lax.Precision.HIGHEST)
    return current

def layer_newton(matrix):
    wide = matrix.astype(jnp.float32)
    squared = jnp.sum(jnp.square(wide))
    current = wide / (jnp.sqrt(squared) + norm_epsilon)
    for iteration in range(NS_ITERS):
        gram_part = jnp.dot(current.T, current, precision=lax.Precision.HIGHEST)
        polynomial = quintic_b * gram_part + quintic_c * jnp.dot(gram_part, gram_part, precision=lax.Precision.HIGHEST)
        current = quintic_a * current + jnp.dot(current, polynomial, precision=lax.Precision.HIGHEST)
    return current

def reference(momentum, grad_one, grad_two):
    momentum_one = (momentum_decay * momentum.astype(jnp.float32) + grad_one.astype(jnp.float32)).astype(jnp.bfloat16)
    momentum_two = (momentum_decay * momentum_one.astype(jnp.float32) + grad_two.astype(jnp.float32)).astype(jnp.bfloat16)
    blocks = momentum_one.reshape(LAYERS * HEADS, HEAD_ROWS, LATENT)
    update_one = block_newton(blocks).reshape(LAYERS, ROWS, LATENT) * jnp.sqrt(jnp.float32(max(HEAD_ROWS, LATENT)))
    layers_out = [layer_newton(momentum_two[index]) for index in range(LAYERS)]
    update_two = jnp.stack(layers_out, axis=0) * jnp.sqrt(jnp.float32(ROWS))
    return (update_one, update_two)
```

```python
import functools
import math

import jax
import jax.numpy as jnp
from jax import lax
from jax.experimental import pallas as pl
from jax.experimental.pallas import tpu as pltpu
from jax.sharding import PartitionSpec as P

HEAD_ROWS = 256
NS_ITERS = 5
ROWS = 32768
TILE = 128

quintic_a = 3.4445
quintic_b = -4.775
quintic_c = 2.0315
norm_epsilon = 1e-07
momentum_decay = 0.95

f32, bf16 = jnp.float32, jnp.bfloat16
VMEM_LIMIT = 48 << 20


def split(value):
    high = value.astype(bf16)
    return high, (value - high.astype(f32)).astype(bf16)


def dot_split(left, right):
    (left_high, left_low), (right_high, right_low) = left, right
    return jnp.dot(
        jnp.concatenate([left_low, left_high, left_high], 1),
        jnp.concatenate([right_high, right_low, right_high], 0),
        preferred_element_type=f32,
    )


def dot_symmetric(left, right):
    (high, low), (right_high, right_low) = left, right
    half = high.shape[0] // 2
    top = dot_split((high[:half], low[:half]), right)
    corner = dot_split((high[half:], low[half:]), (right_high[:, half:], right_low[:, half:]))
    return jnp.concatenate([top, jnp.concatenate([top[:, half:].T, corner], 1)], 0)


def identity(size):
    rows = lax.broadcasted_iota(jnp.int32, (size, size), 0)
    return (rows == lax.broadcasted_iota(jnp.int32, (size, size), 1)).astype(f32)


def gram_newton(grams, dot=dot_split):
    eye = identity(grams[0].shape[0])
    results = None
    for iteration in range(NS_ITERS):
        halves = [split(gram) for gram in grams]
        polynomials = [
            quintic_b * gram + quintic_c * dot(half, half)
            for gram, half in zip(grams, halves)
        ]
        factors = [split(polynomial) for polynomial in polynomials]
        if iteration < NS_ITERS - 1:
            once = [
                quintic_a * gram + dot(half, factor)
                for gram, factor, half in zip(grams, factors, halves)
            ]
            grams = [
                quintic_a * value + dot(split(value), factor)
                for value, factor in zip(once, factors)
            ]
        if results is None:
            results = [polynomial + quintic_a * eye for polynomial in polynomials]
        else:
            results = [
                quintic_a * result + dot(split(result), factor)
                for result, factor in zip(results, factors)
            ]
    return results


def normalizer(gram):
    trace = jnp.sum(gram * identity(gram.shape[0]))
    return 1.0 / (jnp.sqrt(trace) + norm_epsilon)


def momentum_of(momentum, gradient):
    return (momentum_decay * momentum.astype(f32) + gradient.astype(f32)).astype(bf16)


def compiler_params():
    return pltpu.CompilerParams(vmem_limit_bytes=VMEM_LIMIT)


def heads_kernel(count, momentum_ref, grad_ref, *refs):
    update_ref, token_ref = refs[-2:]
    blocks, grams, scales = [], [], []
    for index in range(count):
        block = momentum_of(momentum_ref[index], grad_ref[index])
        gram = lax.dot_general(
            block, block, (((1,), (1,)), ((), ())), preferred_element_type=f32
        )
        scale = normalizer(gram)
        blocks.append(block)
        scales.append(scale)
        grams.append(gram * (scale * scale))
    gain = math.sqrt(max(HEAD_ROWS, momentum_ref.shape[-1]))
    for index, result in enumerate(gram_newton(grams)):
        high, low = split(result * (scales[index] * gain))
        update_ref[index] = jnp.dot(
            jnp.concatenate([low, high], 1),
            jnp.concatenate([blocks[index], blocks[index]], 0),
            preferred_element_type=f32,
        )
    token_ref[...] = jnp.zeros_like(token_ref)


def heads_part(momentum, gradient, update, after, first, last):
    latent = momentum.shape[-1]
    momentum, gradient = [value.reshape(-1, HEAD_ROWS, latent) for value in (momentum, gradient)]
    count = max(size for size in range(1, 5) if first % size == 0 and last % size == 0)
    spec = pl.BlockSpec((count, HEAD_ROWS, latent), lambda step: (step + first // count, 0, 0))
    anywhere = pl.BlockSpec(memory_space=pl.ANY)
    operands, specs, aliases = [momentum, gradient, after], [spec, spec, anywhere], {}
    if update is not None:
        aliases = {len(operands): 0}
        operands.append(update)
        specs.append(anywhere)
    blocks = last - first
    return pl.pallas_call(
        functools.partial(heads_kernel, count),
        grid=(blocks // count,),
        in_specs=specs,
        out_specs=[spec, pl.BlockSpec((1, TILE), lambda step: (0, 0))],
        out_shape=[
            jax.ShapeDtypeStruct(momentum.shape, f32), jax.ShapeDtypeStruct((1, TILE), f32)
        ],
        input_output_aliases=aliases,
        compiler_params=compiler_params(),
        cost_estimate=pl.CostEstimate(
            flops=blocks * 57 * 2 * HEAD_ROWS**3,
            bytes_accessed=blocks * HEAD_ROWS * latent * 8,
            transcendentals=0,
        ),
        name="heads",
    )(*operands)


def tiles_above(latent):
    count = latent // TILE
    return [(row, col) for row in range(count) for col in range(row + 1, count)]


def packed_rows(latent, parts):
    count = latent // TILE
    rows = (len(tiles_above(latent)) + count // 2) * TILE + 8
    return -(-rows // (8 * parts)) * 8 * parts


def tile(index):
    return pl.ds(index * TILE, TILE)


def tile_position():
    shape = (TILE, TILE)
    return lax.broadcasted_iota(jnp.int32, shape, 0), lax.broadcasted_iota(jnp.int32, shape, 1)


def pack(full_ref, packed_ref):
    latent = full_ref.shape[0]
    above = tiles_above(latent)
    row_of, col_of = tile_position()
    diagonals = []
    for index, (row, col) in enumerate(above):
        packed_ref[tile(index), :] = full_ref[tile(row), tile(col)]
    for pair in range(latent // TILE // 2):
        first = full_ref[tile(2 * pair), tile(2 * pair)]
        second = full_ref[tile(2 * pair + 1), tile(2 * pair + 1)]
        packed_ref[tile(len(above) + pair), :] = jnp.where(row_of <= col_of, first, second)
        diagonals.append(jnp.sum(jnp.where(row_of == col_of, second, 0.0), axis=0, keepdims=True))
    start = (len(above) + len(diagonals)) * TILE
    rest = packed_ref.shape[0] - start
    diagonals.append(jnp.zeros((rest - len(diagonals), TILE), f32))
    packed_ref[pl.ds(start, rest), :] = jnp.concatenate(diagonals, 0)


def unpack(packed_ref, full_ref):
    latent = full_ref.shape[0]
    above = tiles_above(latent)
    row_of, col_of = tile_position()
    for index, (row, col) in enumerate(above):
        value = packed_ref[tile(index), :]
        full_ref[tile(row), tile(col)] = value
        full_ref[tile(col), tile(row)] = value.T
    pairs = latent // TILE // 2
    diagonals = packed_ref[pl.ds((len(above) + pairs) * TILE, 8), :]
    for pair in range(pairs):
        value = packed_ref[tile(len(above) + pair), :]
        turned = value.T
        full_ref[tile(2 * pair), tile(2 * pair)] = jnp.where(row_of <= col_of, value, turned)
        second = jnp.where(row_of > col_of, value, turned)
        full_ref[tile(2 * pair + 1), tile(2 * pair + 1)] = jnp.where(
            row_of == col_of, diagonals[pair : pair + 1, :], second
        )


def chunk_rows(rows):
    return math.gcd(rows, 512)


def gram_kernel(
    place_ref, momentum_ref, one_ref, two_ref,
    values_ref, keep_ref, send_ref,
    inputs_ref, results_ref, total_ref, packed_ref, read_sems, write_sems,
):
    team, core = place_ref[0], place_ref[1]
    layers, rows, latent = momentum_ref.shape
    height, half = chunk_rows(rows), latent // 2
    steps = [(layer, start) for layer in range(layers) for start in range(0, rows, height)]

    def read(step, which):
        layer, start = steps[step]
        return pltpu.make_async_copy(
            (momentum_ref, one_ref, two_ref)[which].at[team ^ layer, pl.ds(start, height), :],
            inputs_ref.at[which, step],
            read_sems.at[which, step],
        )

    def write(step):
        layer, start = steps[step]
        return pltpu.make_async_copy(
            results_ref.at[step],
            values_ref.at[layer, pl.ds(start, height), :],
            write_sems.at[step],
        )

    def gram(left, right):
        return lax.dot_general(
            left, right, (((0,), (0,)), ((), ())), preferred_element_type=f32
        )

    for step in range(len(steps)):
        for which in range(3):
            read(step, which).start()
    for step, (layer, start) in enumerate(steps):
        for which in range(3):
            read(step, which).wait()
        first = momentum_of(inputs_ref[0, step], inputs_ref[1, step])
        value = momentum_of(first, inputs_ref[2, step])
        results_ref[step] = value
        write(step).start()
        top = gram(value[:, :half], value)
        low = gram(value[:, half:], value[:, half:])
        if start == 0:
            total_ref[:half, :] = top
            total_ref[half:, half:] = low
        else:
            total_ref[:half, :] += top
            total_ref[half:, half:] += low
        if start + height == rows:
            pack(total_ref, packed_ref)
            size = packed_ref.shape[0] // 2
            keep_ref[layer] = packed_ref[pl.ds(pl.multiple_of(core * size, 8), size), :]
            send_ref[layer] = packed_ref[pl.ds(pl.multiple_of((1 - core) * size, 8), size), :]
    for step in range(len(steps)):
        write(step).wait()


def gram_part(place, momentum, grad_one, grad_two):
    layers, rows, latent = momentum.shape
    height = chunk_rows(rows)
    steps = layers * rows // height
    packed = packed_rows(latent, 2)
    whole = pl.BlockSpec(memory_space=pltpu.VMEM)
    anywhere = pl.BlockSpec(memory_space=pl.ANY)
    half_shape = jax.ShapeDtypeStruct((layers, packed // 2, TILE), f32)
    return pl.pallas_call(
        gram_kernel,
        in_specs=[pl.BlockSpec(memory_space=pltpu.SMEM)] + [anywhere] * 3,
        out_specs=[anywhere, whole, whole],
        out_shape=[jax.ShapeDtypeStruct(momentum.shape, bf16), half_shape, half_shape],
        scratch_shapes=[
            pltpu.VMEM((3, steps, height, latent), bf16),
            pltpu.VMEM((steps, height, latent), bf16),
            pltpu.VMEM((latent, latent), f32),
            pltpu.VMEM((packed, TILE), f32),
            pltpu.SemaphoreType.DMA((3, steps)),
            pltpu.SemaphoreType.DMA((steps,)),
        ],
        compiler_params=compiler_params(),
        cost_estimate=pl.CostEstimate(
            flops=layers * rows * latent * latent * 2,
            bytes_accessed=layers * rows * latent * 8,
            transcendentals=0,
        ),
        name="grams",
    )(place, momentum, grad_one, grad_two)


def join_halves(core, mine, other, packed_ref):
    size = packed_ref.shape[0] // 2
    packed_ref[pl.ds(pl.multiple_of(core * size, 8), size), :] = mine
    packed_ref[pl.ds(pl.multiple_of((1 - core) * size, 8), size), :] = other


def newton_kernel(
    place_ref, mine_ref, other_ref, _, half_ref, high_ref, low_ref, packed_ref, full_ref
):
    core = place_ref[1]
    join_halves(core, mine_ref[...], other_ref[...], packed_ref)
    unpack(packed_ref, full_ref)
    gram = full_ref[...]
    scale = normalizer(gram)
    (result,) = gram_newton([gram * (scale * scale)], dot_symmetric)
    full_ref[...] = result * (scale * math.sqrt(ROWS))
    high, low = split(full_ref[...])
    high_ref[...] = high
    low_ref[...] = low
    pack(full_ref, packed_ref)
    height = half_ref.shape[0]
    half_ref[...] = packed_ref[pl.ds(pl.multiple_of(core * height, 8), height), :]


def newton_part(place, mine, other, after, latent):
    height = mine.shape[0]
    whole = pl.BlockSpec(memory_space=pltpu.VMEM)
    square = jax.ShapeDtypeStruct((latent, latent), bf16)
    return pl.pallas_call(
        newton_kernel,
        in_specs=[
            pl.BlockSpec(memory_space=pltpu.SMEM), whole, whole, pl.BlockSpec(memory_space=pl.ANY)
        ],
        out_specs=[whole] * 3,
        out_shape=[jax.ShapeDtypeStruct(mine.shape, f32), square, square],
        scratch_shapes=[
            pltpu.VMEM((2 * height, TILE), f32),
            pltpu.VMEM((latent, latent), f32),
        ],
        compiler_params=compiler_params(),
        cost_estimate=pl.CostEstimate(
            flops=51 * 2 * latent**3, bytes_accessed=5 * latent**2 * 4, transcendentals=0
        ),
        name="newton",
    )(place, mine, other, after)


def multiply(value, high, low):
    return jnp.dot(value, high, preferred_element_type=f32) + jnp.dot(
        value, low, preferred_element_type=f32
    )


def apply_own_kernel(place_ref, value_ref, high_ref, low_ref, update_ref):
    update_ref[0] = multiply(value_ref[0], high_ref[...], low_ref[...])


def apply_own(place, values, high, low):
    _, rows, latent = values.shape
    height = math.gcd(rows, 256)
    whole = pl.BlockSpec(memory_space=pltpu.VMEM)
    return pl.pallas_call(
        apply_own_kernel,
        grid_spec=pltpu.PrefetchScalarGridSpec(
            num_scalar_prefetch=1,
            grid=(rows // height,),
            in_specs=[
                pl.BlockSpec((1, height, latent), lambda step, place: (0, step, 0)), whole, whole
            ],
            out_specs=pl.BlockSpec((1, height, latent), lambda step, place: (place[0], step, 0)),
        ),
        out_shape=jax.ShapeDtypeStruct(values.shape, f32),
        compiler_params=compiler_params(),
        cost_estimate=pl.CostEstimate(
            flops=rows * latent * latent * 4, bytes_accessed=rows * latent * 6, transcendentals=0
        ),
        name="apply_own",
    )(place, values, high, low)


def apply_kernel(
    place_ref, values_ref, mine_ref, other_ref, _, update_ref,
    inputs_ref, results_ref, packed_ref, full_ref, read_sems, write_sems,
):
    layers, rows, latent = values_ref.shape
    height = chunk_rows(rows)
    steps = [(layer, start) for layer in range(1, layers) for start in range(0, rows, height)]
    team, core = place_ref[0], place_ref[1]

    def read(step):
        layer, start = steps[step]
        return pltpu.make_async_copy(
            values_ref.at[layer, pl.ds(start, height), :], inputs_ref.at[step], read_sems.at[step]
        )

    def write(step):
        layer, start = steps[step]
        return pltpu.make_async_copy(
            results_ref.at[step],
            update_ref.at[team ^ layer, pl.ds(start, height), :],
            write_sems.at[step],
        )

    for step in range(len(steps)):
        read(step).start()
    factors = []
    for layer in range(layers - 1):
        join_halves(core, mine_ref[layer], other_ref[layer], packed_ref.at[layer])
        unpack(packed_ref.at[layer], full_ref.at[layer])
        factors.append(split(full_ref[layer]))
    for step, (layer, _) in enumerate(steps):
        read(step).wait()
        results_ref[step] = multiply(inputs_ref[step], *factors[layer - 1])
        write(step).start()
    for step in range(len(steps)):
        write(step).wait()


def apply_others(place, values, mine, other, update):
    layers, rows, latent = values.shape
    height = chunk_rows(rows)
    steps = (layers - 1) * rows // height
    whole = pl.BlockSpec(memory_space=pltpu.VMEM)
    anywhere = pl.BlockSpec(memory_space=pl.ANY)
    return pl.pallas_call(
        apply_kernel,
        in_specs=[pl.BlockSpec(memory_space=pltpu.SMEM), anywhere, whole, whole, anywhere],
        out_specs=anywhere,
        out_shape=jax.ShapeDtypeStruct(values.shape, f32),
        scratch_shapes=[
            pltpu.VMEM((steps, height, latent), bf16),
            pltpu.VMEM((steps, height, latent), f32),
            pltpu.VMEM((layers - 1, 2 * mine.shape[1], TILE), f32),
            pltpu.VMEM((layers - 1, latent, latent), f32),
            pltpu.SemaphoreType.DMA((steps,)),
            pltpu.SemaphoreType.DMA((steps,)),
        ],
        input_output_aliases={4: 0},
        compiler_params=compiler_params(),
        cost_estimate=pl.CostEstimate(
            flops=(layers - 1) * rows * latent * latent * 4,
            bytes_accessed=(layers - 1) * rows * latent * 6,
            transcendentals=0,
        ),
        name="apply_others",
    )(place, values, mine, other, update)


def shards(layer_size, head_size, momentum, grad_one, grad_two):
    layers, rows, latent = momentum.shape
    head = lax.axis_index("head")
    place = jnp.stack([lax.axis_index("layer"), head % 2]).astype(jnp.int32)

    def to_head(value, distance):
        return lax.ppermute(
            value, "head", [(index, index ^ distance) for index in range(head_size)]
        )

    def to_layer(value, distance):
        return lax.ppermute(
            value, "layer", [(index, index ^ distance) for index in range(layer_size)]
        )

    distances = []
    while 1 << len(distances) < head_size // 2:
        distances.append(2 * ((2 << len(distances)) - 1))

    blocks = layers * rows // HEAD_ROWS
    windows = 2 + len(distances)
    bounds = [blocks * part // windows for part in range(windows + 1)]
    update_one = None

    def heads(part, update, after):
        if bounds[part] == bounds[part + 1]:
            return update, jnp.zeros((1, TILE), f32)
        return heads_part(momentum, grad_one, update, after, bounds[part], bounds[part + 1])

    values, keep, send = gram_part(place, momentum, grad_one, grad_two)
    received = to_head(send, 1)
    sums = [keep[layer] + received[layer] for layer in range(layers)]
    arriving = [to_layer(sums[layer], layer) for layer in range(1, layers)]
    update_one, token = heads(0, None, sums[0])
    total = functools.reduce(jnp.add, arriving, sums[0]) + token
    for part, distance in enumerate(distances):
        arriving = to_head(total, distance)
        update_one, token = heads(1 + part, update_one, total)
        total = (total + arriving) + token
    other = to_head(total, 1)
    half, high, low = newton_part(place, total, other, token, latent)

    factors = [to_layer(half, layer) for layer in range(1, layers)]
    update_one, token = heads(windows - 1, update_one, half)
    mine = jnp.stack(factors) + token
    other = to_head(mine, 1)
    update_two = apply_own(place, values, high, low)
    update_two = apply_others(place, values, mine, other, update_two)
    return update_one.reshape(momentum.shape), update_two


def solution(mesh):
    spec = P(None, ("layer", "head"), None)
    return jax.shard_map(
        functools.partial(shards, mesh.shape["layer"], mesh.shape["head"]),
        mesh=mesh,
        in_specs=(spec, spec, spec),
        out_specs=(spec, spec),
        check_vma=False,
    )
```

```python
import functools
import math

import jax
import jax.numpy as jnp
from jax import lax
from jax.experimental import pallas as pl
from jax.experimental.pallas import tpu as pltpu
from jax.sharding import PartitionSpec as P

HEAD_ROWS = 256
NS_ITERS = 5
ROWS = 32768
TILE = 128

quintic_a = 3.4445
quintic_b = -4.775
quintic_c = 2.0315
norm_epsilon = 1e-07
momentum_decay = 0.95

f32, bf16 = jnp.float32, jnp.bfloat16
VMEM_LIMIT = 32 << 20


def split(value):
    high = value.astype(bf16)
    return high, (value - high.astype(f32)).astype(bf16)


def dot_split(left, right):
    (left_high, left_low), (right_high, right_low) = left, right
    return jnp.dot(
        jnp.concatenate([left_low, left_high, left_high], 1),
        jnp.concatenate([right_high, right_low, right_high], 0),
        preferred_element_type=f32,
    )


def dot_symmetric(left, right):
    (high, low), (right_high, right_low) = left, right
    half = high.shape[0] // 2
    top = dot_split((high[:half], low[:half]), right)
    corner = dot_split((high[half:], low[half:]), (right_high[:, half:], right_low[:, half:]))
    return jnp.concatenate([top, jnp.concatenate([top[:, half:].T, corner], 1)], 0)


def identity(size):
    rows = lax.broadcasted_iota(jnp.int32, (size, size), 0)
    return (rows == lax.broadcasted_iota(jnp.int32, (size, size), 1)).astype(f32)


def gram_newton(grams, dot=dot_split):
    eye = identity(grams[0].shape[0])
    results = None
    for iteration in range(NS_ITERS):
        halves = [split(gram) for gram in grams]
        polynomials = [
            quintic_b * gram + quintic_c * dot(half, half)
            for gram, half in zip(grams, halves)
        ]
        factors = [split(polynomial) for polynomial in polynomials]
        if iteration < NS_ITERS - 1:
            once = [
                quintic_a * gram + dot(half, factor)
                for gram, factor, half in zip(grams, factors, halves)
            ]
            grams = [
                quintic_a * value + dot(split(value), factor)
                for value, factor in zip(once, factors)
            ]
        if results is None:
            results = [polynomial + quintic_a * eye for polynomial in polynomials]
        else:
            results = [
                quintic_a * result + dot(split(result), factor)
                for result, factor in zip(results, factors)
            ]
    return results


def normalizer(gram):
    trace = jnp.sum(gram * identity(gram.shape[0]))
    return 1.0 / (jnp.sqrt(trace) + norm_epsilon)


def momentum_of(momentum, gradient):
    return (momentum_decay * momentum.astype(f32) + gradient.astype(f32)).astype(bf16)


def compiler_params(limit=VMEM_LIMIT):
    return pltpu.CompilerParams(vmem_limit_bytes=limit)


def heads_kernel(first, count, place_ref, blocks_ref, *refs):
    update_ref, token_ref, results_ref, write_sems = refs[-4:]
    per_layer = blocks_ref.shape[1] // HEAD_ROWS
    blocks, grams, scales = [], [], []
    for index in range(first, first + count):
        rows = pl.ds(index % per_layer * HEAD_ROWS, HEAD_ROWS)
        block = blocks_ref[index // per_layer, rows, :]
        gram = lax.dot_general(
            block, block, (((1,), (1,)), ((), ())), preferred_element_type=f32
        )
        scale = normalizer(gram)
        blocks.append(block)
        scales.append(scale)
        grams.append(gram * (scale * scale))
    gain = math.sqrt(max(HEAD_ROWS, blocks_ref.shape[-1]))

    def write(index):
        layer, part = (first + index) // per_layer, (first + index) % per_layer
        return pltpu.make_async_copy(
            results_ref.at[index],
            update_ref.at[place_ref[0] ^ layer, pl.ds(part * HEAD_ROWS, HEAD_ROWS), :],
            write_sems.at[index],
        )

    for index, result in enumerate(gram_newton(grams)):
        high, low = split(result * (scales[index] * gain))
        results_ref[index] = jnp.dot(
            jnp.concatenate([low, high], 1),
            jnp.concatenate([blocks[index], blocks[index]], 0),
            preferred_element_type=f32,
        )
        write(index).start()
    token_ref[...] = jnp.zeros_like(token_ref)
    for index in range(count):
        write(index).wait()


def heads_part(place, blocks, update, after, first, last):
    latent = blocks.shape[-1]
    whole = pl.BlockSpec(memory_space=pltpu.VMEM)
    anywhere = pl.BlockSpec(memory_space=pl.ANY)
    operands, aliases = [place, blocks, after], {}
    if update is not None:
        aliases = {len(operands): 0}
        operands.append(update)
    count = last - first
    return pl.pallas_call(
        functools.partial(heads_kernel, first, count),
        in_specs=[pl.BlockSpec(memory_space=pltpu.SMEM), whole] + [anywhere] * (len(operands) - 2),
        out_specs=[anywhere, whole],
        out_shape=[
            jax.ShapeDtypeStruct(blocks.shape, f32), jax.ShapeDtypeStruct((1, TILE), f32)
        ],
        scratch_shapes=[
            pltpu.VMEM((count, HEAD_ROWS, latent), f32),
            pltpu.SemaphoreType.DMA((count,)),
        ],
        input_output_aliases=aliases,
        compiler_params=compiler_params(),
        cost_estimate=pl.CostEstimate(
            flops=count * 57 * 2 * HEAD_ROWS**3,
            bytes_accessed=count * HEAD_ROWS * latent * 8,
            transcendentals=0,
        ),
        name="heads",
    )(*operands)


def tiles_above(latent):
    count = latent // TILE
    return [(row, col) for row in range(count) for col in range(row + 1, count)]


def packed_rows(latent, parts):
    count = latent // TILE
    rows = (len(tiles_above(latent)) + count // 2) * TILE + 8
    return -(-rows // (8 * parts)) * 8 * parts


def tile(index):
    return pl.ds(index * TILE, TILE)


def tile_position():
    shape = (TILE, TILE)
    return lax.broadcasted_iota(jnp.int32, shape, 0), lax.broadcasted_iota(jnp.int32, shape, 1)


def pack(full_ref, packed_ref):
    latent = full_ref.shape[0]
    above = tiles_above(latent)
    row_of, col_of = tile_position()
    diagonals = []
    for index, (row, col) in enumerate(above):
        packed_ref[tile(index), :] = full_ref[tile(row), tile(col)]
    for pair in range(latent // TILE // 2):
        first = full_ref[tile(2 * pair), tile(2 * pair)]
        second = full_ref[tile(2 * pair + 1), tile(2 * pair + 1)]
        packed_ref[tile(len(above) + pair), :] = jnp.where(row_of <= col_of, first, second)
        diagonals.append(jnp.sum(jnp.where(row_of == col_of, second, 0.0), axis=0, keepdims=True))
    start = (len(above) + len(diagonals)) * TILE
    rest = packed_ref.shape[0] - start
    diagonals.append(jnp.zeros((rest - len(diagonals), TILE), f32))
    packed_ref[pl.ds(start, rest), :] = jnp.concatenate(diagonals, 0)


def unpack(packed_ref, full_ref):
    latent = full_ref.shape[0]
    above = tiles_above(latent)
    row_of, col_of = tile_position()
    for index, (row, col) in enumerate(above):
        value = packed_ref[tile(index), :]
        full_ref[tile(row), tile(col)] = value
        full_ref[tile(col), tile(row)] = value.T
    pairs = latent // TILE // 2
    diagonals = packed_ref[pl.ds((len(above) + pairs) * TILE, 8), :]
    for pair in range(pairs):
        value = packed_ref[tile(len(above) + pair), :]
        turned = value.T
        full_ref[tile(2 * pair), tile(2 * pair)] = jnp.where(row_of <= col_of, value, turned)
        second = jnp.where(row_of > col_of, value, turned)
        full_ref[tile(2 * pair + 1), tile(2 * pair + 1)] = jnp.where(
            row_of == col_of, diagonals[pair : pair + 1, :], second
        )


def chunk_rows(rows):
    return math.gcd(rows, 512)


def gram_kernel(
    place_ref, momentum_ref, one_ref, two_ref,
    first_ref, second_ref, keep_ref, send_ref,
    inputs_ref, total_ref, packed_ref, read_sems,
):
    team, core = place_ref[0], place_ref[1]
    layers, rows, latent = momentum_ref.shape
    height, half = chunk_rows(rows), latent // 2
    steps = [(layer, start) for layer in range(layers) for start in range(0, rows, height)]

    def read(step, which):
        layer, start = steps[step]
        return pltpu.make_async_copy(
            (momentum_ref, one_ref, two_ref)[which].at[team ^ layer, pl.ds(start, height), :],
            inputs_ref.at[which, step],
            read_sems.at[which, step],
        )

    def gram(left, right):
        return lax.dot_general(
            left, right, (((0,), (0,)), ((), ())), preferred_element_type=f32
        )

    for step in range(len(steps)):
        for which in range(3):
            read(step, which).start()
    for step, (layer, start) in enumerate(steps):
        for which in range(3):
            read(step, which).wait()
        first = momentum_of(inputs_ref[0, step], inputs_ref[1, step])
        value = momentum_of(first, inputs_ref[2, step])
        first_ref[layer, pl.ds(start, height), :] = first
        second_ref[layer, pl.ds(start, height), :] = value
        top = gram(value[:, :half], value)
        low = gram(value[:, half:], value[:, half:])
        if start == 0:
            total_ref[:half, :] = top
            total_ref[half:, half:] = low
        else:
            total_ref[:half, :] += top
            total_ref[half:, half:] += low
        if start + height == rows:
            pack(total_ref, packed_ref)
            size = packed_ref.shape[0] // 2
            keep_ref[layer] = packed_ref[pl.ds(pl.multiple_of(core * size, 8), size), :]
            send_ref[layer] = packed_ref[pl.ds(pl.multiple_of((1 - core) * size, 8), size), :]


def gram_part(place, momentum, grad_one, grad_two):
    layers, rows, latent = momentum.shape
    height = chunk_rows(rows)
    steps = layers * rows // height
    packed = packed_rows(latent, 2)
    whole = pl.BlockSpec(memory_space=pltpu.VMEM)
    anywhere = pl.BlockSpec(memory_space=pl.ANY)
    half_shape = jax.ShapeDtypeStruct((layers, packed // 2, TILE), f32)
    rows_shape = jax.ShapeDtypeStruct(momentum.shape, bf16)
    return pl.pallas_call(
        gram_kernel,
        in_specs=[pl.BlockSpec(memory_space=pltpu.SMEM)] + [anywhere] * 3,
        out_specs=[whole] * 4,
        out_shape=[rows_shape, rows_shape, half_shape, half_shape],
        scratch_shapes=[
            pltpu.VMEM((3, steps, height, latent), bf16),
            pltpu.VMEM((latent, latent), f32),
            pltpu.VMEM((packed, TILE), f32),
            pltpu.SemaphoreType.DMA((3, steps)),
        ],
        compiler_params=compiler_params(44 << 20),
        cost_estimate=pl.CostEstimate(
            flops=layers * rows * latent * latent * 2,
            bytes_accessed=layers * rows * latent * 6,
            transcendentals=0,
        ),
        name="grams",
    )(place, momentum, grad_one, grad_two)


def join_halves(core, mine, other, packed_ref):
    size = packed_ref.shape[0] // 2
    packed_ref[pl.ds(pl.multiple_of(core * size, 8), size), :] = mine
    packed_ref[pl.ds(pl.multiple_of((1 - core) * size, 8), size), :] = other


def newton_kernel(
    place_ref, mine_ref, other_ref, _, half_ref, high_ref, low_ref, packed_ref, full_ref
):
    core = place_ref[1]
    join_halves(core, mine_ref[...], other_ref[...], packed_ref)
    unpack(packed_ref, full_ref)
    gram = full_ref[...]
    scale = normalizer(gram)
    (result,) = gram_newton([gram * (scale * scale)], dot_symmetric)
    full_ref[...] = result * (scale * math.sqrt(ROWS))
    high, low = split(full_ref[...])
    high_ref[...] = high
    low_ref[...] = low
    pack(full_ref, packed_ref)
    height = half_ref.shape[0]
    half_ref[...] = packed_ref[pl.ds(pl.multiple_of(core * height, 8), height), :]


def newton_part(place, mine, other, after, latent):
    height = mine.shape[0]
    whole = pl.BlockSpec(memory_space=pltpu.VMEM)
    square = jax.ShapeDtypeStruct((latent, latent), bf16)
    return pl.pallas_call(
        newton_kernel,
        in_specs=[
            pl.BlockSpec(memory_space=pltpu.SMEM), whole, whole, pl.BlockSpec(memory_space=pl.ANY)
        ],
        out_specs=[whole] * 3,
        out_shape=[jax.ShapeDtypeStruct(mine.shape, f32), square, square],
        scratch_shapes=[
            pltpu.VMEM((2 * height, TILE), f32),
            pltpu.VMEM((latent, latent), f32),
        ],
        compiler_params=compiler_params(),
        cost_estimate=pl.CostEstimate(
            flops=51 * 2 * latent**3, bytes_accessed=5 * latent**2 * 4, transcendentals=0
        ),
        name="newton",
    )(place, mine, other, after)


def multiply(value, high, low):
    return jnp.dot(
        jnp.concatenate([value, value], 1),
        jnp.concatenate([low, high], 0),
        preferred_element_type=f32,
    )


def apply_kernel(layers, own, place_ref, values_ref, *refs):
    factor_refs, (update_ref, results_ref, *scratch, write_sems) = refs[:2], refs[2 if own else 3 :]
    rows = values_ref.shape[1]
    height = math.gcd(rows, 256)
    steps = [(index, start) for index in range(len(layers)) for start in range(0, rows, height)]
    team, core = place_ref[0], place_ref[1]

    def write(step):
        index, start = steps[step]
        return pltpu.make_async_copy(
            results_ref.at[step],
            update_ref.at[team ^ layers[index], pl.ds(start, height), :],
            write_sems.at[step],
        )

    if own:
        factors = [(factor_refs[0][...], factor_refs[1][...])]
    else:
        factors = []
        packed_ref, full_ref = scratch
        for index in range(len(layers)):
            join_halves(core, factor_refs[0][index], factor_refs[1][index], packed_ref.at[index])
            unpack(packed_ref.at[index], full_ref.at[index])
            factors.append(split(full_ref[index]))
    for step, (index, start) in enumerate(steps):
        value = values_ref[layers[index], pl.ds(start, height), :]
        results_ref[step] = multiply(value, *factors[index])
        write(step).start()
    for step in range(len(steps)):
        write(step).wait()


def apply_part(place, values, layers, factors, update):
    _, rows, latent = values.shape
    height = math.gcd(rows, 256)
    steps = len(layers) * rows // height
    whole = pl.BlockSpec(memory_space=pltpu.VMEM)
    anywhere = pl.BlockSpec(memory_space=pl.ANY)
    operands, specs, scratch, aliases = [place, values, *factors], [whole] * 3, [], {}
    own = update is None
    if not own:
        aliases = {len(operands): 0}
        operands.append(update)
        specs.append(anywhere)
        scratch = [
            pltpu.VMEM((len(layers), 2 * factors[0].shape[1], TILE), f32),
            pltpu.VMEM((len(layers), latent, latent), f32),
        ]
    return pl.pallas_call(
        functools.partial(apply_kernel, layers, own),
        in_specs=[pl.BlockSpec(memory_space=pltpu.SMEM)] + specs,
        out_specs=anywhere,
        out_shape=jax.ShapeDtypeStruct(values.shape, f32),
        scratch_shapes=[pltpu.VMEM((steps, height, latent), f32)]
        + scratch
        + [pltpu.SemaphoreType.DMA((steps,))],
        input_output_aliases=aliases,
        compiler_params=compiler_params(),
        cost_estimate=pl.CostEstimate(
            flops=len(layers) * rows * latent * latent * 4,
            bytes_accessed=len(layers) * rows * latent * 6,
            transcendentals=0,
        ),
        name="apply",
    )(*operands)


def shards(layer_size, head_size, momentum, grad_one, grad_two):
    layers, rows, latent = momentum.shape
    head = lax.axis_index("head")
    place = jnp.stack([lax.axis_index("layer"), head % 2]).astype(jnp.int32)

    def to_head(value, distance):
        return lax.ppermute(
            value, "head", [(index, index ^ distance) for index in range(head_size)]
        )

    def to_layer(value, distance):
        return lax.ppermute(
            value, "layer", [(index, index ^ distance) for index in range(layer_size)]
        )

    distances = []
    while 1 << len(distances) < head_size // 2:
        distances.append(2 * ((2 << len(distances)) - 1))

    blocks = layers * rows // HEAD_ROWS
    windows = 2 + len(distances)
    weights = [5, 3] + [4] * (len(distances) - 1) + [4]
    bounds = [blocks * sum(weights[:part]) // sum(weights) for part in range(windows + 1)]
    update_one = None

    def heads(part, update, after):
        if bounds[part] == bounds[part + 1]:
            return update, jnp.zeros((1, TILE), f32)
        return heads_part(place, first, update, after, bounds[part], bounds[part + 1])

    first, values, keep, send = gram_part(place, momentum, grad_one, grad_two)
    received = to_head(send, 1)
    sums = [keep[layer] + received[layer] for layer in range(layers)]
    arriving = [to_layer(sums[layer], layer) for layer in range(1, layers)]
    update_one, token = heads(0, None, sums[0])
    total = functools.reduce(jnp.add, arriving, sums[0]) + token
    for part, distance in enumerate(distances):
        arriving = to_head(total, distance)
        update_one, token = heads(1 + part, update_one, total)
        total = (total + arriving) + token
    other = to_head(total, 1)
    half, high, low = newton_part(place, total, other, token, latent)

    factors = [to_layer(half, layer) for layer in range(1, layers)]
    update_one, token = heads(windows - 1, update_one, half)
    mine = jnp.stack(factors) + token
    other = to_head(mine, 1)
    update_two = apply_part(place, values, (0,), [high, low], None)
    update_two = apply_part(place, values, tuple(range(1, layers)), [mine, other], update_two)
    return update_one, update_two


def solution(mesh):
    spec = P(None, ("layer", "head"), None)
    return jax.shard_map(
        functools.partial(shards, mesh.shape["layer"], mesh.shape["head"]),
        mesh=mesh,
        in_specs=(spec, spec, spec),
        out_specs=(spec, spec),
        check_vma=False,
    )
```

```python
import functools
import math

import jax
import jax.numpy as jnp
from jax import lax
from jax.experimental import pallas as pl
from jax.experimental.pallas import tpu as pltpu
from jax.sharding import PartitionSpec as P

HEAD_ROWS = 256
NS_ITERS = 5
ROWS = 32768
TILE = 128

quintic_a = 3.4445
quintic_b = -4.775
quintic_c = 2.0315
norm_epsilon = 1e-07
momentum_decay = 0.95

f32, bf16 = jnp.float32, jnp.bfloat16
VMEM_LIMIT = 32 << 20


def split(value):
    high = value.astype(bf16)
    return high, (value - high.astype(f32)).astype(bf16)


def dot_split(left, right):
    (left_high, left_low), (right_high, right_low) = left, right
    return jnp.dot(
        jnp.concatenate([left_low, left_high, left_high], 1),
        jnp.concatenate([right_high, right_low, right_high], 0),
        preferred_element_type=f32,
    )


def dot_symmetric(left, right):
    (high, low), (right_high, right_low) = left, right
    half = high.shape[0] // 2
    top = dot_split((high[:half], low[:half]), right)
    corner = dot_split((high[half:], low[half:]), (right_high[:, half:], right_low[:, half:]))
    return jnp.concatenate([top, jnp.concatenate([top[:, half:].T, corner], 1)], 0)


def identity(size):
    rows = lax.broadcasted_iota(jnp.int32, (size, size), 0)
    return (rows == lax.broadcasted_iota(jnp.int32, (size, size), 1)).astype(f32)


def gram_newton(grams, dot=dot_split):
    eye = identity(grams[0].shape[0])
    results = None
    for iteration in range(NS_ITERS):
        halves = [split(gram) for gram in grams]
        polynomials = [
            quintic_b * gram + quintic_c * dot(half, half)
            for gram, half in zip(grams, halves)
        ]
        factors = [split(polynomial) for polynomial in polynomials]
        if iteration < NS_ITERS - 1:
            once = [
                quintic_a * gram + dot(half, factor)
                for gram, factor, half in zip(grams, factors, halves)
            ]
            grams = [
                quintic_a * value + dot(split(value), factor)
                for value, factor in zip(once, factors)
            ]
        if results is None:
            results = [polynomial + quintic_a * eye for polynomial in polynomials]
        else:
            results = [
                quintic_a * result + dot(split(result), factor)
                for result, factor in zip(results, factors)
            ]
    return results


def normalizer(gram):
    trace = jnp.sum(gram * identity(gram.shape[0]))
    return 1.0 / (jnp.sqrt(trace) + norm_epsilon)


def momentum_of(momentum, gradient):
    return (momentum_decay * momentum.astype(f32) + gradient.astype(f32)).astype(bf16)


def compiler_params(limit=VMEM_LIMIT):
    return pltpu.CompilerParams(vmem_limit_bytes=limit)


def heads_kernel(first, count, place_ref, blocks_ref, *refs):
    update_ref, token_ref, results_ref, write_sems = refs[-4:]
    per_layer = blocks_ref.shape[1] // HEAD_ROWS
    blocks, grams, scales = [], [], []
    for index in range(first, first + count):
        rows = pl.ds(index % per_layer * HEAD_ROWS, HEAD_ROWS)
        block = blocks_ref[index // per_layer, rows, :]
        gram = lax.dot_general(
            block, block, (((1,), (1,)), ((), ())), preferred_element_type=f32
        )
        scale = normalizer(gram)
        blocks.append(block)
        scales.append(scale)
        grams.append(gram * (scale * scale))
    gain = math.sqrt(max(HEAD_ROWS, blocks_ref.shape[-1]))

    def write(index):
        layer, part = (first + index) // per_layer, (first + index) % per_layer
        return pltpu.make_async_copy(
            results_ref.at[index],
            update_ref.at[place_ref[0] ^ layer, pl.ds(part * HEAD_ROWS, HEAD_ROWS), :],
            write_sems.at[index],
        )

    for index, result in enumerate(gram_newton(grams)):
        high, low = split(result * (scales[index] * gain))
        results_ref[index] = jnp.dot(
            jnp.concatenate([low, high], 1),
            jnp.concatenate([blocks[index], blocks[index]], 0),
            preferred_element_type=f32,
        )
        write(index).start()
    token_ref[...] = jnp.zeros_like(token_ref)
    for index in range(count):
        write(index).wait()


def heads_part(place, blocks, update, after, first, last):
    latent = blocks.shape[-1]
    whole = pl.BlockSpec(memory_space=pltpu.VMEM)
    anywhere = pl.BlockSpec(memory_space=pl.ANY)
    operands, aliases = [place, blocks, after], {}
    if update is not None:
        aliases = {len(operands): 0}
        operands.append(update)
    count = last - first
    return pl.pallas_call(
        functools.partial(heads_kernel, first, count),
        in_specs=[pl.BlockSpec(memory_space=pltpu.SMEM), whole] + [anywhere] * (len(operands) - 2),
        out_specs=[anywhere, whole],
        out_shape=[
            jax.ShapeDtypeStruct(blocks.shape, f32), jax.ShapeDtypeStruct((1, TILE), f32)
        ],
        scratch_shapes=[
            pltpu.VMEM((count, HEAD_ROWS, latent), f32),
            pltpu.SemaphoreType.DMA((count,)),
        ],
        input_output_aliases=aliases,
        compiler_params=compiler_params(),
        cost_estimate=pl.CostEstimate(
            flops=count * 57 * 2 * HEAD_ROWS**3,
            bytes_accessed=count * HEAD_ROWS * latent * 8,
            transcendentals=0,
        ),
        name="heads",
    )(*operands)


def tiles_above(latent):
    count = latent // TILE
    return [(row, col) for row in range(count) for col in range(row + 1, count)]


def packed_rows(latent, parts):
    count = latent // TILE
    rows = (len(tiles_above(latent)) + count // 2) * TILE + 8
    return -(-rows // (8 * parts)) * 8 * parts


def tile(index):
    return pl.ds(index * TILE, TILE)


def tile_position():
    shape = (TILE, TILE)
    return lax.broadcasted_iota(jnp.int32, shape, 0), lax.broadcasted_iota(jnp.int32, shape, 1)


def pack(full_ref, packed_ref):
    latent = full_ref.shape[0]
    above = tiles_above(latent)
    row_of, col_of = tile_position()
    diagonals = []
    for index, (row, col) in enumerate(above):
        packed_ref[tile(index), :] = full_ref[tile(row), tile(col)]
    for pair in range(latent // TILE // 2):
        first = full_ref[tile(2 * pair), tile(2 * pair)]
        second = full_ref[tile(2 * pair + 1), tile(2 * pair + 1)]
        packed_ref[tile(len(above) + pair), :] = jnp.where(row_of <= col_of, first, second)
        diagonals.append(jnp.sum(jnp.where(row_of == col_of, second, 0.0), axis=0, keepdims=True))
    start = (len(above) + len(diagonals)) * TILE
    rest = packed_ref.shape[0] - start
    diagonals.append(jnp.zeros((rest - len(diagonals), TILE), f32))
    packed_ref[pl.ds(start, rest), :] = jnp.concatenate(diagonals, 0)


def unpack(packed_ref, full_ref):
    latent = full_ref.shape[0]
    above = tiles_above(latent)
    row_of, col_of = tile_position()
    for index, (row, col) in enumerate(above):
        value = packed_ref[tile(index), :]
        full_ref[tile(row), tile(col)] = value
        full_ref[tile(col), tile(row)] = value.T
    pairs = latent // TILE // 2
    diagonals = packed_ref[pl.ds((len(above) + pairs) * TILE, 8), :]
    for pair in range(pairs):
        value = packed_ref[tile(len(above) + pair), :]
        turned = value.T
        full_ref[tile(2 * pair), tile(2 * pair)] = jnp.where(row_of <= col_of, value, turned)
        second = jnp.where(row_of > col_of, value, turned)
        full_ref[tile(2 * pair + 1), tile(2 * pair + 1)] = jnp.where(
            row_of == col_of, diagonals[pair : pair + 1, :], second
        )


def chunk_rows(rows):
    return math.gcd(rows, 512)


def gram_kernel(
    place_ref, momentum_ref, one_ref, two_ref,
    first_ref, second_ref, keep_ref, send_ref,
    inputs_ref, total_ref, packed_ref, read_sems,
):
    team, core = place_ref[0], place_ref[1]
    layers, rows, latent = momentum_ref.shape
    height, half = chunk_rows(rows), latent // 2
    steps = [(layer, start) for layer in range(layers) for start in range(0, rows, height)]

    def read(step, which):
        layer, start = steps[step]
        return pltpu.make_async_copy(
            (momentum_ref, one_ref, two_ref)[which].at[team ^ layer, pl.ds(start, height), :],
            inputs_ref.at[which, step],
            read_sems.at[which, step],
        )

    def gram(left, right):
        return lax.dot_general(
            left, right, (((0,), (0,)), ((), ())), preferred_element_type=f32
        )

    for step in range(len(steps)):
        for which in range(3):
            read(step, which).start()
    for step, (layer, start) in enumerate(steps):
        for which in range(3):
            read(step, which).wait()
        first = momentum_of(inputs_ref[0, step], inputs_ref[1, step])
        value = momentum_of(first, inputs_ref[2, step])
        first_ref[layer, pl.ds(start, height), :] = first
        second_ref[layer, pl.ds(start, height), :] = value
        top = gram(value[:, :half], value)
        low = gram(value[:, half:], value[:, half:])
        if start == 0:
            total_ref[:half, :] = top
            total_ref[half:, half:] = low
        else:
            total_ref[:half, :] += top
            total_ref[half:, half:] += low
        if start + height == rows:
            pack(total_ref, packed_ref)
            size = packed_ref.shape[0] // 2
            keep_ref[layer] = packed_ref[pl.ds(pl.multiple_of(core * size, 8), size), :]
            send_ref[layer] = packed_ref[pl.ds(pl.multiple_of((1 - core) * size, 8), size), :]


def gram_part(place, momentum, grad_one, grad_two):
    layers, rows, latent = momentum.shape
    height = chunk_rows(rows)
    steps = layers * rows // height
    packed = packed_rows(latent, 2)
    whole = pl.BlockSpec(memory_space=pltpu.VMEM)
    anywhere = pl.BlockSpec(memory_space=pl.ANY)
    half_shape = jax.ShapeDtypeStruct((layers, packed // 2, TILE), f32)
    rows_shape = jax.ShapeDtypeStruct(momentum.shape, bf16)
    return pl.pallas_call(
        gram_kernel,
        in_specs=[pl.BlockSpec(memory_space=pltpu.SMEM)] + [anywhere] * 3,
        out_specs=[whole] * 4,
        out_shape=[rows_shape, rows_shape, half_shape, half_shape],
        scratch_shapes=[
            pltpu.VMEM((3, steps, height, latent), bf16),
            pltpu.VMEM((latent, latent), f32),
            pltpu.VMEM((packed, TILE), f32),
            pltpu.SemaphoreType.DMA((3, steps)),
        ],
        compiler_params=compiler_params(44 << 20),
        cost_estimate=pl.CostEstimate(
            flops=layers * rows * latent * latent * 2,
            bytes_accessed=layers * rows * latent * 6,
            transcendentals=0,
        ),
        name="grams",
    )(place, momentum, grad_one, grad_two)


def join_halves(core, mine, other, packed_ref):
    size = packed_ref.shape[0] // 2
    packed_ref[pl.ds(pl.multiple_of(core * size, 8), size), :] = mine
    packed_ref[pl.ds(pl.multiple_of((1 - core) * size, 8), size), :] = other


def newton_kernel(
    place_ref, mine_ref, other_ref, _, half_ref, high_ref, low_ref, packed_ref, full_ref
):
    core = place_ref[1]
    join_halves(core, mine_ref[...], other_ref[...], packed_ref)
    unpack(packed_ref, full_ref)
    gram = full_ref[...]
    scale = normalizer(gram)
    (result,) = gram_newton([gram * (scale * scale)], dot_symmetric)
    full_ref[...] = result * (scale * math.sqrt(ROWS))
    high, low = split(full_ref[...])
    high_ref[...] = high
    low_ref[...] = low
    pack(full_ref, packed_ref)
    height = half_ref.shape[0]
    half_ref[...] = packed_ref[pl.ds(pl.multiple_of(core * height, 8), height), :]


def newton_part(place, mine, other, after, latent):
    height = mine.shape[0]
    whole = pl.BlockSpec(memory_space=pltpu.VMEM)
    square = jax.ShapeDtypeStruct((latent, latent), bf16)
    return pl.pallas_call(
        newton_kernel,
        in_specs=[
            pl.BlockSpec(memory_space=pltpu.SMEM), whole, whole, pl.BlockSpec(memory_space=pl.ANY)
        ],
        out_specs=[whole] * 3,
        out_shape=[jax.ShapeDtypeStruct(mine.shape, f32), square, square],
        scratch_shapes=[
            pltpu.VMEM((2 * height, TILE), f32),
            pltpu.VMEM((latent, latent), f32),
        ],
        compiler_params=compiler_params(),
        cost_estimate=pl.CostEstimate(
            flops=51 * 2 * latent**3, bytes_accessed=5 * latent**2 * 4, transcendentals=0
        ),
        name="newton",
    )(place, mine, other, after)


def multiply(value, high, low):
    return jnp.dot(
        jnp.concatenate([value, value], 1),
        jnp.concatenate([low, high], 0),
        preferred_element_type=f32,
    )


def apply_kernel(layers, own, place_ref, values_ref, *refs):
    factor_refs, (update_ref, results_ref, *scratch, write_sems) = refs[:2], refs[2 if own else 3 :]
    rows = values_ref.shape[1]
    height = math.gcd(rows, 256)
    steps = [(index, start) for index in range(len(layers)) for start in range(0, rows, height)]
    team, core = place_ref[0], place_ref[1]

    def write(step):
        index, start = steps[step]
        return pltpu.make_async_copy(
            results_ref.at[step],
            update_ref.at[team ^ layers[index], pl.ds(start, height), :],
            write_sems.at[step],
        )

    def factor(index):
        if own:
            return factor_refs[0][...], factor_refs[1][...]
        packed_ref, full_ref = scratch
        join_halves(core, factor_refs[0][index], factor_refs[1][index], packed_ref.at[index])
        unpack(packed_ref.at[index], full_ref.at[index])
        return split(full_ref[index])

    for step, (index, start) in enumerate(steps):
        if start == 0:
            current = factor(index)
        value = values_ref[layers[index], pl.ds(start, height), :]
        results_ref[step] = multiply(value, *current)
        write(step).start()
    for step in range(len(steps)):
        write(step).wait()


def apply_part(place, values, layers, factors, update):
    _, rows, latent = values.shape
    height = math.gcd(rows, 256)
    steps = len(layers) * rows // height
    whole = pl.BlockSpec(memory_space=pltpu.VMEM)
    anywhere = pl.BlockSpec(memory_space=pl.ANY)
    operands, specs, scratch, aliases = [place, values, *factors], [whole] * 3, [], {}
    own = update is None
    if not own:
        aliases = {len(operands): 0}
        operands.append(update)
        specs.append(anywhere)
        scratch = [
            pltpu.VMEM((len(layers), 2 * factors[0].shape[1], TILE), f32),
            pltpu.VMEM((len(layers), latent, latent), f32),
        ]
    return pl.pallas_call(
        functools.partial(apply_kernel, layers, own),
        in_specs=[pl.BlockSpec(memory_space=pltpu.SMEM)] + specs,
        out_specs=anywhere,
        out_shape=jax.ShapeDtypeStruct(values.shape, f32),
        scratch_shapes=[pltpu.VMEM((steps, height, latent), f32)]
        + scratch
        + [pltpu.SemaphoreType.DMA((steps,))],
        input_output_aliases=aliases,
        compiler_params=compiler_params(),
        cost_estimate=pl.CostEstimate(
            flops=len(layers) * rows * latent * latent * 4,
            bytes_accessed=len(layers) * rows * latent * 6,
            transcendentals=0,
        ),
        name="apply",
    )(*operands)


def shards(layer_size, head_size, momentum, grad_one, grad_two):
    layers, rows, latent = momentum.shape
    head = lax.axis_index("head")
    place = jnp.stack([lax.axis_index("layer"), head % 2]).astype(jnp.int32)

    def to_head(value, distance):
        return lax.ppermute(
            value, "head", [(index, index ^ distance) for index in range(head_size)]
        )

    def to_layer(value, distance):
        return lax.ppermute(
            value, "layer", [(index, index ^ distance) for index in range(layer_size)]
        )

    distances = []
    while 1 << len(distances) < head_size // 2:
        distances.append(2 * ((2 << len(distances)) - 1))

    blocks = layers * rows // HEAD_ROWS
    windows = 2 + len(distances)
    weights = [5, 3] + [4] * (len(distances) - 1) + [4]
    bounds = [blocks * sum(weights[:part]) // sum(weights) for part in range(windows + 1)]
    update_one = None

    def heads(part, update, after):
        if bounds[part] == bounds[part + 1]:
            return update, jnp.zeros((1, TILE), f32)
        return heads_part(place, first, update, after, bounds[part], bounds[part + 1])

    first, values, keep, send = gram_part(place, momentum, grad_one, grad_two)
    received = to_head(send, 1)
    sums = [keep[layer] + received[layer] for layer in range(layers)]
    arriving = [to_layer(sums[layer], layer) for layer in range(1, layers)]
    update_one, token = heads(0, None, sums[0])
    total = functools.reduce(jnp.add, arriving, sums[0]) + token
    for part, distance in enumerate(distances):
        arriving = to_head(total, distance)
        update_one, token = heads(1 + part, update_one, total)
        total = (total + arriving) + token
    other = to_head(total, 1)
    half, high, low = newton_part(place, total, other, token, latent)

    factors = [to_layer(half, layer) for layer in range(1, layers)]
    update_one, token = heads(windows - 1, update_one, half)
    mine = jnp.stack(factors) + token
    other = to_head(mine, 1)
    update_two = apply_part(place, values, (0,), [high, low], None)
    update_two = apply_part(place, values, tuple(range(1, layers)), [mine, other], update_two)
    return update_one, update_two


def solution(mesh):
    spec = P(None, ("layer", "head"), None)
    return jax.shard_map(
        functools.partial(shards, mesh.shape["layer"], mesh.shape["head"]),
        mesh=mesh,
        in_specs=(spec, spec, spec),
        out_specs=(spec, spec),
        check_vma=False,
    )
```
